32 devices in a mesh: dp: 2 (over core), tensor: 16 (over z, y, x).
Axes of the slice: x: 2, y: 2, z: 4, core: 2. Of those that a mesh axis runs over, the one named last changes fastest.
Arguments:
- gate_pre: bfloat16 [1024, 16384], P('dp', 'tensor'), may hold values from -6 to 6
- up_pre: bfloat16 [1024, 16384], P('dp', 'tensor'), may hold values from -6 to 6
- down_weight: bfloat16 [16384, 4096], P('tensor'), may hold values from -0.0625 to 0.0625
- block_mask: int32 [128, 32], P('tensor'), may hold values from 0 to 1, as said below
- out_grad: bfloat16 [1024, 4096], P(('dp', 'tensor')), may hold values from -6 to 6
Outputs:
- layer_out: bfloat16 [1024, 4096], P(('dp', 'tensor'))
- gate_grad: bfloat16 [1024, 16384], P('dp', 'tensor')
- up_grad: bfloat16 [1024, 16384], P('dp', 'tensor')
- weight_grad: bfloat16 [16384, 4096], P('tensor')
The draws below stay inside these ranges and needn't reach their ends.
Inputs may be any that keep to these rules, and one draw needn't show every extreme that they name: `block_mask`: each tensor shard's 8 x 32 blocks hold between 64 and 192 kept blocks; in every draw some shard keeps exactly 192.
All inputs are finite; a program needn't handle non-finite values.
Results may differ from the reference program's by a relative error of at most 0.0049.
Values may be sent and summed in bfloat16 or wider, within the bound.
A program may use at most 128 MiB of HBM per device.

```python
import math
import jax
import jax.numpy as jnp

D = 4096
FF = 16384
TOKENS = 1024
SHARDS = 16
NB_F = 128
NB_D = 32
BLOCKS_SHARD = 256
KEEP_MAX = 192
KEEP_LO = 64


def draw_block_mask(key, part):
    shard_keys = jax.random.split(jax.random.fold_in(key, 11), SHARDS)

    def shard_ranks(single):
        return jax.random.permutation(single, BLOCKS_SHARD)
    ranks = jax.vmap(shard_ranks)(shard_keys)
    counts = jax.random.randint(jax.random.fold_in(key, 12), (SHARDS,), KEEP_LO, KEEP_MAX + 1)
    busiest = jax.random.randint(jax.random.fold_in(key, 13), (), 0, SHARDS)
    counts = jnp.where(jnp.arange(SHARDS) == busiest, KEEP_MAX, counts)
    flags = (ranks < counts[:, None]).astype(jnp.int32)
    return flags.reshape(NB_F, NB_D)


def block_scale(key, dims, pieces, low, top_value):
    factor_of = 1.0
    for axis_at, shards_of in pieces:
        heights = jax.random.uniform(jax.random.fold_in(jax.random.fold_in(key, 6), axis_at), (shards_of,), jnp.float32, low / len(pieces), top_value / len(pieces))
        factor_of = factor_of * jnp.repeat(jnp.exp(heights), dims[axis_at] // shards_of).reshape((-1,) + (1,) * (len(dims) - 1 - axis_at))
    return factor_of


def bell_draw(stream_key, shape, spread, reach, cuts=(), kind=jnp.bfloat16):
    gain = block_scale(stream_key, shape, cuts, -0.22, 0.18) if cuts else 1.0
    values = jax.random.normal(stream_key, shape, jnp.float32) * spread * gain
    return jnp.minimum(jnp.maximum(values, -reach), reach).astype(kind)


def setup_inputs(seed: int = 0) -> dict:
    arg_keys = jax.random.split(jax.random.key(seed), 6)
    gate_pre = bell_draw(arg_keys[0], (TOKENS, FF), 1.0, 6.0, ((0, 2), (1, 16)))
    up_pre = bell_draw(arg_keys[1], (TOKENS, FF), 1.0, 6.0, ((0, 2), (1, 16)))
    down_weight = bell_draw(arg_keys[2], (FF, D), (FF // 2) ** -0.5, 0.0625, ((0, 16),))
    block_mask = draw_block_mask(jax.random.fold_in(arg_keys[5], 71), 0)
    out_grad = bell_draw(arg_keys[4], (TOKENS, D), 1.0, 6.0, ((0, 32),))
    return {"gate_pre": gate_pre, "up_pre": up_pre, "down_weight": down_weight, "block_mask": block_mask, "out_grad": out_grad}


def expand_mask(matrix, mask):
    nbf, nbd = mask.shape
    blocks = matrix.reshape(nbf, 128, nbd, 128) * mask.astype(matrix.dtype)[:, None, :, None]
    return blocks.reshape(nbf * 128, nbd * 128)

def reference(gate_pre, up_pre, down_weight, block_mask, out_grad):
    masked = expand_mask(down_weight, block_mask)
    gate_val = gate_pre.astype(jnp.float32)
    up_val = up_pre.astype(jnp.float32)
    sigmoid_gate = jax.nn.sigmoid(gate_val)
    silu_gate = gate_val * sigmoid_gate
    hidden = (silu_gate * up_val).astype(jnp.bfloat16)
    layer_out = jnp.dot(hidden, masked, preferred_element_type=jnp.float32).astype(jnp.bfloat16)
    hidden_grad = jnp.dot(out_grad, masked.T, preferred_element_type=jnp.float32)
    gate_grad = (hidden_grad * up_val * sigmoid_gate * (1.0 + gate_val * (1.0 - sigmoid_gate))).astype(jnp.bfloat16)
    up_grad = (hidden_grad * silu_gate).astype(jnp.bfloat16)
    grad_scale = 1.0 / math.sqrt(TOKENS)
    total = jnp.dot(hidden.T, out_grad, preferred_element_type=jnp.float32) * grad_scale
    weight_grad = expand_mask(total, block_mask.astype(jnp.float32)).astype(jnp.bfloat16)
    return (layer_out, gate_grad, up_grad, weight_grad)
```

```python
import functools
import math

import jax
import jax.numpy as jnp
from jax import lax
from jax.experimental import pallas as pl
from jax.experimental.pallas import tpu as pltpu
from jax.sharding import PartitionSpec as P

BLOCK = 128
ORDER = (0, 1, 3, 2)


def remote(src, dst, sends, recvs, at, device):
    return pltpu.make_async_remote_copy(
        src_ref=src,
        dst_ref=dst,
        send_sem=sends.at[at],
        recv_sem=recvs.at[at],
        device_id=device,
        device_id_type=pl.DeviceIdType.MESH,
    )


def fused_kernel(
    scale,
    gate_hbm, up_hbm, weight_hbm, mask_ref, grad_hbm,
    out_hbm, gate_grad_hbm, up_grad_hbm, weight_grad_hbm,
    gate, up, weight, cot, hidden, hidden_t, partial,
    first, second, third, send_second, send_third, final, gate_grad, up_grad, tile_out,
    in_sem, out_sem, tile_sem,
    z_send, z_recv, hop1_send, hop1_recv, hop2_send, hop2_recv, core_send, core_recv,
    sum1_send, sum1_recv, sum2_send, sum2_recv, sum3_send, sum3_recv,
):
    d = lax.axis_index("dp")
    t = lax.axis_index("tensor")
    x = t % 2
    y = (t // 2) % 2
    z = t // 4
    ff, width = weight.shape
    tokens = gate.shape[0]
    half = width // 2
    halves = (pl.ds(0, half), pl.ds(half, half))
    zs = [z] + [(z + k) % 4 for k in (1, 2, 3)]
    x_peer = {"tensor": z * 4 + y * 2 + (1 - x)}
    y_peer = {"tensor": z * 4 + (1 - y) * 2 + x}
    core_peer = {"dp": 1 - d}
    z_peer = [None] + [{"tensor": zs[k] * 4 + y * 2 + x} for k in (1, 2, 3)]

    loads = [
        pltpu.make_async_copy(gate_hbm, gate, in_sem.at[0]),
        pltpu.make_async_copy(up_hbm, up, in_sem.at[1]),
        pltpu.make_async_copy(weight_hbm.at[:, halves[0]], weight.at[:, halves[0]], in_sem.at[2]),
        pltpu.make_async_copy(weight_hbm.at[:, halves[1]], weight.at[:, halves[1]], in_sem.at[3]),
        pltpu.make_async_copy(grad_hbm, cot.at[d, z, y, x], in_sem.at[4]),
    ]
    for copy in loads:
        copy.start()

    barrier = pltpu.get_barrier_semaphore()
    peers = [x_peer, y_peer, core_peer] + z_peer[1:]
    for peer in peers:
        pl.semaphore_signal(barrier, inc=1, device_id=peer, device_id_type=pl.DeviceIdType.MESH)
    pl.semaphore_wait(barrier, len(peers))

    along_z = {}
    for k in (1, 3, 2):
        along_z[k] = remote(grad_hbm, cot.at[d, z, y, x], z_send, z_recv, k - 1, z_peer[k])
        along_z[k].start()
    hop1, hop2, to_core = {}, {}, {}

    def start_hop1(k):
        at = zs[(4 - k) % 4]
        for h, peer in enumerate((x_peer, y_peer)):
            dst = cot.at[d, at, y, x, :, halves[h]]
            src = grad_hbm.at[:, halves[h]] if k == 0 else dst
            hop1[k, h] = remote(src, dst, hop1_send, hop1_recv, 2 * k + h, peer)
            hop1[k, h].start()

    def start_hop2(k):
        at = zs[(4 - k) % 4]
        refs = (cot.at[d, at, y, :, :, halves[0]], cot.at[d, at, :, x, :, halves[1]])
        for h, peer in enumerate((y_peer, x_peer)):
            hop1[k, h].wait_recv()
        for h, peer in enumerate((y_peer, x_peer)):
            hop2[k, h] = remote(refs[h], refs[h], hop2_send, hop2_recv, 2 * k + h, peer)
            hop2[k, h].start()

    def start_core(k):
        at = zs[(4 - k) % 4]
        for h in range(2):
            hop2[k, h].wait_recv()
        to_core[k] = remote(cot.at[d, at], cot.at[d, at], core_send, core_recv, k, core_peer)
        to_core[k].start()

    start_hop1(0)

    loads[0].wait()
    loads[1].wait()

    def hidden_step(step, _):
        cols = pl.ds(pl.multiple_of(step * 128, 128), 128)
        g = gate[:, cols].astype(jnp.float32)
        u = up[:, cols].astype(jnp.float32)
        value = g * jax.nn.sigmoid(g) * u
        hidden[:, cols] = value.astype(jnp.bfloat16)
        hidden_t[d, cols, :] = value.T.astype(jnp.bfloat16)
        return 0

    lax.fori_loop(0, ff // 128, hidden_step, 0)
    hidden_core = remote(hidden_t.at[d], hidden_t.at[d], core_send, core_recv, 4, core_peer)
    hidden_core.start()

    def forward(h):
        wide = 512

        def step(i, _):
            cols = pl.ds(pl.multiple_of(h * half + i * wide, wide), wide)
            for b in range(ff // BLOCK):
                rows = pl.ds(b * BLOCK, BLOCK)
                keep = jnp.broadcast_to(mask_ref[b : b + 1, cols], (BLOCK, wide))
                weight[rows, cols] = weight[rows, cols] * keep.astype(jnp.bfloat16)
            part = jnp.dot(hidden[...], weight[:, cols], preferred_element_type=jnp.float32)
            partial[:, :, :, :, cols] = part.astype(jnp.bfloat16).reshape(
                partial.shape[:4] + (wide,)
            )
            return 0

        lax.fori_loop(0, half // wide, step, 0)

    sum1, sum2, sum3 = {}, {}, {}

    def start_sum1(h):
        for k in (1, 3, 2, 0):
            at = zs[k]
            src = (partial.at[at, :, 1 - x, :, halves[0]], partial.at[at, 1 - y, :, :, halves[1]])[h]
            sum1[k, h] = remote(
                src, first.at[h, k], sum1_send, sum1_recv, 2 * k + h, (x_peer, y_peer)[h]
            )
            sum1[k, h].start()

    loads[2].wait()
    forward(0)
    start_sum1(0)
    for k in (1, 3):
        along_z[k].wait_recv()
        start_hop1(k)
    loads[3].wait()
    forward(1)
    start_sum1(1)
    along_z[2].wait_recv()
    start_hop1(2)
    loads[4].wait()
    for k in ORDER:
        start_hop2(k)

    for k in (1, 3, 2, 0):
        at = zs[k]
        for h in range(2):
            sum1[k, h].wait_recv()
            other = (1 - y, 1 - x)[h]
            mine = (partial[at, 1 - y, x, :, halves[0]], partial[at, y, 1 - x, :, halves[1]])[h]
            total = mine.astype(jnp.float32) + first[h, k, other].astype(jnp.float32)
            send_second[h, k] = total.astype(jnp.bfloat16)
            sum2[k, h] = remote(
                send_second.at[h, k], second.at[h, k], sum2_send, sum2_recv, 2 * k + h,
                (y_peer, x_peer)[h],
            )
            sum2[k, h].start()

    for k in ORDER:
        start_core(k)

    def own_total(k, h):
        mine = partial[zs[k], y, x, :, halves[h]].astype(jnp.float32)
        near = first[h, k, (y, x)[h]].astype(jnp.float32)
        return mine + near + second[h, k].astype(jnp.float32)

    for k in (1, 3, 2):
        for h in range(2):
            sum2[k, h].wait_recv()
            send_third[h, k - 1] = own_total(k, h).astype(jnp.bfloat16)
            sum3[k, h] = remote(
                send_third.at[h, k - 1], third.at[h, k - 1], sum3_send, sum3_recv, 2 * k + h - 2,
                z_peer[k],
            )
            sum3[k, h].start()

    def grad_step(i, _):
        wide = 256
        rows = pl.ds(pl.multiple_of(i * wide, wide), wide)
        rows_out = cot[d].reshape(tokens, width)
        back = lax.dot_general(
            rows_out, weight[rows, :], (((1,), (1,)), ((), ())), preferred_element_type=jnp.float32
        )
        g = gate[:, rows].astype(jnp.float32)
        u = up[:, rows].astype(jnp.float32)
        s = jax.nn.sigmoid(g)
        gate_grad[:, rows] = (back * u * s * (1.0 + g * (1.0 - s))).astype(jnp.bfloat16)
        up_grad[:, rows] = (back * (g * s)).astype(jnp.bfloat16)
        return 0

    lax.fori_loop(0, ff // 256, grad_step, 0)
    stores = [
        pltpu.make_async_copy(gate_grad, gate_grad_hbm, out_sem.at[0]),
        pltpu.make_async_copy(up_grad, up_grad_hbm, out_sem.at[1]),
    ]
    for copy in stores:
        copy.start()

    hidden_core.wait_recv()
    for k in ORDER:
        to_core[k].wait_recv()

    wide = 512

    def tile_copy(slot, i):
        cols = pl.ds(pl.multiple_of(i * wide, wide), wide)
        return pltpu.make_async_copy(
            tile_out.at[slot], weight_grad_hbm.at[:, cols], tile_sem.at[slot]
        )

    def weight_step(j, _):
        for slot in range(2):
            i = 2 * j + slot
            cols = pl.ds(pl.multiple_of(i * wide, wide), wide)

            @pl.when(j > 0)
            def _():
                tile_copy(slot, i - 2).wait()

            total = jnp.zeros((ff, wide), jnp.float32)
            for core in range(2):
                total = total + jnp.dot(
                    hidden_t[core],
                    cot[core, :, :, :, :, cols].reshape(tokens, wide),
                    preferred_element_type=jnp.float32,
                )
            for b in range(ff // BLOCK):
                keep = mask_ref[b : b + 1, cols] * scale
                tile_out[slot, pl.ds(b * BLOCK, BLOCK), :] = (
                    total[b * BLOCK : (b + 1) * BLOCK] * keep
                ).astype(jnp.bfloat16)
            tile_copy(slot, i).start()
        return 0

    steps = width // wide
    lax.fori_loop(0, steps // 2, weight_step, 0)

    for h in range(2):
        sum2[0, h].wait_recv()
        total = own_total(0, h)
        for k in (1, 2, 3):
            sum3[k, h].wait_recv()
            total = total + third[h, k - 1].astype(jnp.float32)
        final[:, halves[h]] = total.astype(jnp.bfloat16)
    stores.append(pltpu.make_async_copy(final, out_hbm, out_sem.at[2]))
    stores[-1].start()

    for copies in (along_z, hop1, hop2, to_core, sum1, sum2, sum3):
        for copy in copies.values():
            copy.wait_send()
    hidden_core.wait_send()
    for copy in stores:
        copy.wait()
    tile_copy(0, steps - 2).wait()
    tile_copy(1, steps - 1).wait()


def fused(gate_pre, up_pre, down_weight, block_mask, out_grad):
    tokens, ff = gate_pre.shape
    rows, width = out_grad.shape
    half = width // 2
    scale = 1.0 / math.sqrt(tokens * 2)
    mask_rows = jnp.repeat(block_mask.astype(jnp.float32), BLOCK, axis=1)
    hbm = pl.BlockSpec(memory_space=pl.ANY)
    bf16 = jnp.bfloat16
    dma = pltpu.SemaphoreType.DMA
    counts = [3, 8, 8, 5, 8, 8, 6]
    return pl.pallas_call(
        functools.partial(fused_kernel, scale),
        out_shape=(
            jax.ShapeDtypeStruct((rows, width), bf16),
            jax.ShapeDtypeStruct((tokens, ff), bf16),
            jax.ShapeDtypeStruct((tokens, ff), bf16),
            jax.ShapeDtypeStruct((ff, width), bf16),
        ),
        in_specs=[hbm, hbm, hbm, pl.BlockSpec(memory_space=pltpu.VMEM), hbm],
        out_specs=(hbm,) * 4,
        scratch_shapes=[
            pltpu.VMEM((tokens, ff), bf16),
            pltpu.VMEM((tokens, ff), bf16),
            pltpu.VMEM((ff, width), bf16),
            pltpu.VMEM((2, 4, 2, 2, rows, width), bf16),
            pltpu.VMEM((tokens, ff), bf16),
            pltpu.VMEM((2, ff, tokens), bf16),
            pltpu.VMEM((4, 2, 2, rows, width), bf16),
            pltpu.VMEM((2, 4, 2, rows, half), bf16),
            pltpu.VMEM((2, 4, rows, half), bf16),
            pltpu.VMEM((2, 3, rows, half), bf16),
            pltpu.VMEM((2, 4, rows, half), bf16),
            pltpu.VMEM((2, 3, rows, half), bf16),
            pltpu.VMEM((rows, width), bf16),
            pltpu.VMEM((tokens, ff), bf16),
            pltpu.VMEM((tokens, ff), bf16),
            pltpu.VMEM((2, ff, 512), bf16),
            dma((5,)),
            dma((3,)),
            dma((2,)),
        ]
        + [dma((count,)) for count in counts for _ in range(2)],
        compiler_params=pltpu.CompilerParams(
            collective_id=0, has_side_effects=True, vmem_limit_bytes=60 * 2**20
        ),
        cost_estimate=pl.CostEstimate(
            flops=8 * tokens * ff * width, bytes_accessed=40 * 2**20, transcendentals=2 * tokens * ff
        ),
    )(gate_pre, up_pre, down_weight, mask_rows, out_grad)


def local(gate_pre, up_pre, down_weight, block_mask, out_grad):
    blk_rows, blk_cols = block_mask.shape
    ff_local, width = down_weight.shape
    masked = (
        down_weight.reshape(blk_rows, 128, blk_cols, 128)
        * block_mask.astype(jnp.bfloat16)[:, None, :, None]
    ).reshape(ff_local, width)
    gate_val = gate_pre.astype(jnp.float32)
    up_val = up_pre.astype(jnp.float32)
    sigmoid_gate = jax.nn.sigmoid(gate_val)
    silu_gate = gate_val * sigmoid_gate
    hidden = (silu_gate * up_val).astype(jnp.bfloat16)
    layer_out = lax.psum_scatter(
        jnp.dot(hidden, masked, preferred_element_type=jnp.float32),
        "tensor",
        scatter_dimension=0,
        tiled=True,
    ).astype(jnp.bfloat16)
    cot_rows = lax.all_gather(out_grad, "tensor", axis=0, tiled=True)
    hidden_grad = lax.dot_general(
        cot_rows, masked, (((1,), (1,)), ((), ())), preferred_element_type=jnp.float32
    )
    gate_grad = (
        hidden_grad * up_val * sigmoid_gate * (1.0 + gate_val * (1.0 - sigmoid_gate))
    ).astype(jnp.bfloat16)
    up_grad = (hidden_grad * silu_gate).astype(jnp.bfloat16)
    tokens_all = out_grad.shape[0] * lax.axis_size("tensor") * lax.axis_size("dp")
    grad_scale = 1.0 / math.sqrt(tokens_all)
    partial_grad = (
        lax.dot_general(
            hidden, cot_rows, (((0,), (0,)), ((), ())), preferred_element_type=jnp.float32
        )
        * grad_scale
    )
    blocked = (
        partial_grad.reshape(blk_rows, 128, blk_cols, 128)
        * block_mask.astype(jnp.float32)[:, None, :, None]
    )
    summed = lax.psum(blocked.reshape(ff_local, width), "dp")
    weight_grad = summed.astype(jnp.bfloat16)
    return (layer_out, gate_grad, up_grad, weight_grad)


def solution(mesh):
    grouped = mesh.shape["dp"] == 2 and mesh.shape["tensor"] == 16
    return jax.shard_map(
        fused if grouped else local,
        mesh=mesh,
        in_specs=(
            P("dp", "tensor"),
            P("dp", "tensor"),
            P("tensor", None),
            P("tensor", None),
            P(("dp", "tensor"), None),
        ),
        out_specs=(
            P(("dp", "tensor"), None),
            P("dp", "tensor"),
            P("dp", "tensor"),
            P("tensor", None),
        ),
        check_vma=False,
    )
```

```python
import functools
import math

import jax
import jax.numpy as jnp
from jax import lax
from jax.experimental import pallas as pl
from jax.experimental.pallas import tpu as pltpu
from jax.sharding import PartitionSpec as P

BLOCK = 128
ORDER = (0, 1, 3, 2)
REST = 8


def remote(src, dst, sends, recvs, at, device):
    return pltpu.make_async_remote_copy(
        src_ref=src,
        dst_ref=dst,
        send_sem=sends.at[at],
        recv_sem=recvs.at[at],
        device_id=device,
        device_id_type=pl.DeviceIdType.MESH,
    )


def fused_kernel(
    scale,
    gate_hbm, up_hbm, weight_hbm, mask_ref, grad_hbm,
    out_hbm, gate_grad_hbm, up_grad_hbm, weight_grad_hbm,
    gate, up, weight, cot, hidden, hidden_t, partial,
    first, second, third, send_second, send_third, final,
    rest_third, rest_second, rest_first, send_rest_second, send_rest_first, gate_grad, up_grad, tile_out,
    in_sem, out_sem, tile_sem,
    z_send, z_recv, hop1_send, hop1_recv, hop2_send, hop2_recv, core_send, core_recv,
    sum1_send, sum1_recv, sum2_send, sum2_recv, sum3_send, sum3_recv,
    rest_send, rest_recv, back_send, back_recv,
):
    d = lax.axis_index("dp")
    t = lax.axis_index("tensor")
    x = t % 2
    y = (t // 2) % 2
    z = t // 4
    ff, width = weight.shape
    tokens = gate.shape[0]
    rest = width // REST
    half = (width - rest) // 2
    halves = (pl.ds(0, half), pl.ds(half, half))
    both, last = pl.ds(0, 2 * half), pl.ds(2 * half, rest)
    zs = [z] + [(z + k) % 4 for k in (1, 2, 3)]
    x_peer = {"tensor": z * 4 + y * 2 + (1 - x)}
    y_peer = {"tensor": z * 4 + (1 - y) * 2 + x}
    core_peer = {"dp": 1 - d}
    z_peer = [None] + [{"tensor": zs[k] * 4 + y * 2 + x} for k in (1, 2, 3)]

    loads = [
        pltpu.make_async_copy(gate_hbm, gate, in_sem.at[0]),
        pltpu.make_async_copy(up_hbm, up, in_sem.at[1]),
        pltpu.make_async_copy(weight_hbm.at[:, last], weight.at[:, last], in_sem.at[2]),
        pltpu.make_async_copy(weight_hbm.at[:, both], weight.at[:, both], in_sem.at[3]),
        pltpu.make_async_copy(grad_hbm, cot.at[d, z, y, x], in_sem.at[4]),
    ]
    for copy in loads:
        copy.start()

    barrier = pltpu.get_barrier_semaphore()
    peers = [x_peer, y_peer, core_peer] + z_peer[1:]
    for peer in peers:
        pl.semaphore_signal(barrier, inc=1, device_id=peer, device_id_type=pl.DeviceIdType.MESH)
    pl.semaphore_wait(barrier, len(peers))

    rest_x = remote(
        grad_hbm.at[:, last], cot.at[d, z, y, x, :, last], rest_send, rest_recv, 0, x_peer
    )
    rest_x.start()
    rest_z = {}
    along_z = {}
    for k in (1, 3, 2):
        along_z[k] = remote(
            grad_hbm.at[:, both], cot.at[d, z, y, x, :, both], z_send, z_recv, k - 1, z_peer[k]
        )
        along_z[k].start()
    hop1, hop2, to_core = {}, {}, {}

    def start_hop1(k):
        at = zs[(4 - k) % 4]
        for h, peer in enumerate((x_peer, y_peer)):
            dst = cot.at[d, at, y, x, :, halves[h]]
            src = grad_hbm.at[:, halves[h]] if k == 0 else dst
            hop1[k, h] = remote(src, dst, hop1_send, hop1_recv, 2 * k + h, peer)
            hop1[k, h].start()

    def start_hop2(k):
        at = zs[(4 - k) % 4]
        refs = (cot.at[d, at, y, :, :, halves[0]], cot.at[d, at, :, x, :, halves[1]])
        for h, peer in enumerate((y_peer, x_peer)):
            hop1[k, h].wait_recv()
        for h, peer in enumerate((y_peer, x_peer)):
            hop2[k, h] = remote(refs[h], refs[h], hop2_send, hop2_recv, 2 * k + h, peer)
            hop2[k, h].start()

    def start_core(k):
        at = zs[(4 - k) % 4]
        for h in range(2):
            hop2[k, h].wait_recv()
        if k:
            rest_z[k].wait_recv()
        to_core[k] = remote(cot.at[d, at], cot.at[d, at], core_send, core_recv, k, core_peer)
        to_core[k].start()

    start_hop1(0)

    loads[0].wait()
    loads[1].wait()

    def hidden_step(step, _):
        cols = pl.ds(pl.multiple_of(step * 128, 128), 128)
        g = gate[:, cols].astype(jnp.float32)
        u = up[:, cols].astype(jnp.float32)
        value = g * jax.nn.sigmoid(g) * u
        hidden[:, cols] = value.astype(jnp.bfloat16)
        hidden_t[d, cols, :] = value.T.astype(jnp.bfloat16)
        return 0

    lax.fori_loop(0, ff // 128, hidden_step, 0)
    hidden_core = remote(hidden_t.at[d], hidden_t.at[d], core_send, core_recv, 4, core_peer)
    hidden_core.start()

    def forward(base, size):
        wide = 256

        def step(i, _):
            cols = pl.ds(pl.multiple_of(base + i * wide, BLOCK), wide)
            for b in range(ff // BLOCK):
                rows = pl.ds(b * BLOCK, BLOCK)
                for c in range(wide // BLOCK):
                    at = pl.ds(pl.multiple_of(base + i * wide + c * BLOCK, BLOCK), BLOCK)
                    keep = mask_ref[b, base // BLOCK + i * (wide // BLOCK) + c]
                    keep = jnp.full((BLOCK, BLOCK), keep.astype(jnp.float32)).astype(jnp.bfloat16)
                    weight[rows, at] = weight[rows, at] * keep
            part = jnp.dot(hidden[...], weight[:, cols], preferred_element_type=jnp.float32)
            partial[:, :, :, :, cols] = part.astype(jnp.bfloat16).reshape(
                partial.shape[:4] + (wide,)
            )
            return 0

        lax.fori_loop(0, size // wide, step, 0)

    sum1, sum2, sum3 = {}, {}, {}

    def start_sum1(h):
        for k in (1, 3, 2, 0):
            at = zs[k]
            src = (partial.at[at, :, 1 - x, :, halves[0]], partial.at[at, 1 - y, :, :, halves[1]])[h]
            sum1[k, h] = remote(
                src, first.at[h, k], sum1_send, sum1_recv, 2 * k + h, (x_peer, y_peer)[h]
            )
            sum1[k, h].start()

    back_z = {}

    def rest_sum(row, column):
        total = partial[z, row, column, :, last].astype(jnp.float32)
        for k in (1, 2, 3):
            total = total + rest_third[k - 1, row, column].astype(jnp.float32)
        return total

    loads[4].wait()
    rest_x.wait_recv()
    rest_y = remote(
        cot.at[d, z, y, :, :, last], cot.at[d, z, y, :, :, last], rest_send, rest_recv, 1, y_peer
    )
    rest_y.start()
    loads[2].wait()
    forward(2 * half, rest)
    for k in (1, 3, 2):
        back_z[k] = remote(
            partial.at[zs[k], :, :, :, last], rest_third.at[k - 1], back_send, back_recv, k - 1,
            z_peer[k],
        )
        back_z[k].start()
    loads[3].wait()
    forward(0, half)
    start_sum1(0)
    rest_y.wait_recv()
    for k in (1, 3, 2):
        rest_z[k] = remote(
            cot.at[d, z, :, :, :, last], cot.at[d, z, :, :, :, last], rest_send, rest_recv, k + 1,
            z_peer[k],
        )
        rest_z[k].start()
    for k in (1, 3):
        along_z[k].wait_recv()
        start_hop1(k)
    forward(half, half)
    start_sum1(1)
    along_z[2].wait_recv()
    start_hop1(2)

    def start_sum2(k):
        at = zs[k]
        for h in range(2):
            sum1[k, h].wait_recv()
            other = (1 - y, 1 - x)[h]
            mine = (partial[at, 1 - y, x, :, halves[0]], partial[at, y, 1 - x, :, halves[1]])[h]
            total = mine.astype(jnp.float32) + first[h, k, other].astype(jnp.float32)
            send_second[h, k] = total.astype(jnp.bfloat16)
            sum2[k, h] = remote(
                send_second.at[h, k], second.at[h, k], sum2_send, sum2_recv, 2 * k + h,
                (y_peer, x_peer)[h],
            )
            sum2[k, h].start()

    start_hop2(0)
    start_hop2(1)
    start_sum2(1)
    start_hop2(3)
    start_sum2(3)
    start_hop2(2)
    start_sum2(2)
    start_sum2(0)
    for k in (1, 2, 3):
        back_z[k].wait_recv()
    for column in range(2):
        send_rest_second[column] = rest_sum(1 - y, column).astype(jnp.bfloat16)
    back_y = remote(send_rest_second, rest_second, back_send, back_recv, 3, y_peer)
    back_y.start()

    def own_total(k, h):
        mine = partial[zs[k], y, x, :, halves[h]].astype(jnp.float32)
        near = first[h, k, (y, x)[h]].astype(jnp.float32)
        return mine + near + second[h, k].astype(jnp.float32)

    def start_sum3(k):
        for h in range(2):
            sum2[k, h].wait_recv()
            send_third[h, k - 1] = own_total(k, h).astype(jnp.bfloat16)
            sum3[k, h] = remote(
                send_third.at[h, k - 1], third.at[h, k - 1], sum3_send, sum3_recv, 2 * k + h - 2,
                z_peer[k],
            )
            sum3[k, h].start()

    start_sum3(1)
    start_core(0)
    start_core(1)
    start_sum3(3)
    back_y.wait_recv()
    total = rest_sum(y, 1 - x) + rest_second[1 - x].astype(jnp.float32)
    send_rest_first[...] = total.astype(jnp.bfloat16)
    back_x = remote(send_rest_first, rest_first, back_send, back_recv, 4, x_peer)
    back_x.start()
    start_core(3)
    start_sum3(2)
    start_core(2)

    def grad_step(i, _):
        wide = 256
        rows = pl.ds(pl.multiple_of(i * wide, wide), wide)
        rows_out = cot[d].reshape(tokens, width)
        back = lax.dot_general(
            rows_out, weight[rows, :], (((1,), (1,)), ((), ())), preferred_element_type=jnp.float32
        )
        g = gate[:, rows].astype(jnp.float32)
        u = up[:, rows].astype(jnp.float32)
        s = jax.nn.sigmoid(g)
        gate_grad[:, rows] = (back * u * s * (1.0 + g * (1.0 - s))).astype(jnp.bfloat16)
        up_grad[:, rows] = (back * (g * s)).astype(jnp.bfloat16)
        return 0

    lax.fori_loop(0, ff // 256, grad_step, 0)
    stores = [
        pltpu.make_async_copy(gate_grad, gate_grad_hbm, out_sem.at[0]),
        pltpu.make_async_copy(up_grad, up_grad_hbm, out_sem.at[1]),
    ]
    for copy in stores:
        copy.start()

    hidden_core.wait_recv()
    for k in ORDER:
        to_core[k].wait_recv()

    wide = 512

    def tile_copy(slot, i):
        cols = pl.ds(pl.multiple_of(i * wide, wide), wide)
        return pltpu.make_async_copy(
            tile_out.at[slot], weight_grad_hbm.at[:, cols], tile_sem.at[slot]
        )

    def weight_step(j, _):
        for slot in range(2):
            i = 2 * j + slot
            cols = pl.ds(pl.multiple_of(i * wide, wide), wide)

            @pl.when(j > 0)
            def _():
                tile_copy(slot, i - 2).wait()

            total = jnp.zeros((ff, wide), jnp.float32)
            for core in range(2):
                total = total + jnp.dot(
                    hidden_t[core],
                    cot[core, :, :, :, :, cols].reshape(tokens, wide),
                    preferred_element_type=jnp.float32,
                )
            for b in range(ff // BLOCK):
                for c in range(wide // BLOCK):
                    keep = mask_ref[b, i * (wide // BLOCK) + c].astype(jnp.float32) * scale
                    block = total[b * BLOCK : (b + 1) * BLOCK, c * BLOCK : (c + 1) * BLOCK]
                    tile_out[slot, pl.ds(b * BLOCK, BLOCK), pl.ds(c * BLOCK, BLOCK)] = (
                        block * keep
                    ).astype(jnp.bfloat16)
            tile_copy(slot, i).start()
        return 0

    steps = width // wide
    lax.fori_loop(0, steps // 2, weight_step, 0)

    for h in range(2):
        sum2[0, h].wait_recv()
        total = own_total(0, h)
        for k in (1, 2, 3):
            sum3[k, h].wait_recv()
            total = total + third[h, k - 1].astype(jnp.float32)
        final[:, halves[h]] = total.astype(jnp.bfloat16)
    back_x.wait_recv()
    total = rest_sum(y, x) + rest_second[x].astype(jnp.float32) + rest_first[...].astype(jnp.float32)
    final[:, last] = total.astype(jnp.bfloat16)
    stores.append(pltpu.make_async_copy(final, out_hbm, out_sem.at[2]))
    stores[-1].start()

    for copies in (along_z, hop1, hop2, to_core, sum1, sum2, sum3, rest_z, back_z):
        for copy in copies.values():
            copy.wait_send()
    for copy in (hidden_core, rest_x, rest_y, back_y, back_x):
        copy.wait_send()
    for copy in stores:
        copy.wait()
    tile_copy(0, steps - 2).wait()
    tile_copy(1, steps - 1).wait()


def fused(gate_pre, up_pre, down_weight, block_mask, out_grad):
    tokens, ff = gate_pre.shape
    rows, width = out_grad.shape
    rest = width // REST
    half = (width - rest) // 2
    scale = 1.0 / math.sqrt(tokens * 2)
    hbm = pl.BlockSpec(memory_space=pl.ANY)
    bf16 = jnp.bfloat16
    dma = pltpu.SemaphoreType.DMA
    counts = [3, 8, 8, 5, 8, 8, 6, 5, 5]
    results = pl.pallas_call(
        functools.partial(fused_kernel, scale),
        out_shape=(
            jax.ShapeDtypeStruct((rows, width), bf16),
            jax.ShapeDtypeStruct((tokens, ff), bf16),
            jax.ShapeDtypeStruct((tokens, ff), bf16),
            jax.ShapeDtypeStruct((ff, width), bf16),
        ),
        in_specs=[hbm, hbm, hbm, pl.BlockSpec(memory_space=pltpu.SMEM), hbm],
        out_specs=(hbm,) * 4,
        scratch_shapes=[
            pltpu.VMEM((tokens, ff), bf16),
            pltpu.VMEM((tokens, ff), bf16),
            pltpu.VMEM((ff, width), bf16),
            pltpu.VMEM((2, 4, 2, 2, rows, width), bf16),
            pltpu.VMEM((tokens, ff), bf16),
            pltpu.VMEM((2, ff, tokens), bf16),
            pltpu.VMEM((4, 2, 2, rows, width), bf16),
            pltpu.VMEM((2, 4, 2, rows, half), bf16),
            pltpu.VMEM((2, 4, rows, half), bf16),
            pltpu.VMEM((2, 3, rows, half), bf16),
            pltpu.VMEM((2, 4, rows, half), bf16),
            pltpu.VMEM((2, 3, rows, half), bf16),
            pltpu.VMEM((rows, width), bf16),
            pltpu.VMEM((3, 2, 2, rows, rest), bf16),
            pltpu.VMEM((2, rows, rest), bf16),
            pltpu.VMEM((rows, rest), bf16),
            pltpu.VMEM((2, rows, rest), bf16),
            pltpu.VMEM((rows, rest), bf16),
            pltpu.VMEM((tokens, ff), bf16),
            pltpu.VMEM((tokens, ff), bf16),
            pltpu.VMEM((2, ff, 512), bf16),
            dma((5,)),
            dma((3,)),
            dma((2,)),
        ]
        + [dma((count,)) for count in counts for _ in range(2)],
        compiler_params=pltpu.CompilerParams(
            collective_id=0, has_side_effects=True, vmem_limit_bytes=60 * 2**20
        ),
        cost_estimate=pl.CostEstimate(
            flops=8 * tokens * ff * width, bytes_accessed=40 * 2**20, transcendentals=2 * tokens * ff
        ),
    )(gate_pre, up_pre, down_weight, block_mask, out_grad)
    return hand_on(results)


def pieces_of(array):
    count = max(1, array.size // 2**19)
    return [(piece * (array.shape[0] // count), array.shape[0] // count) for piece in range(count)]


def hand_on_kernel(arrays, *refs):
    srcs, dsts = refs[:arrays], refs[arrays : 2 * arrays]
    held = refs[2 * arrays : 3 * arrays]
    load_sem, store_sem = refs[3 * arrays :]
    loads, stores = [], []
    for src, dst, hold in zip(srcs, dsts, held):
        for first_row, rows in pieces_of(src):
            at = pl.ds(first_row, rows)
            n = len(loads)
            loads.append(pltpu.make_async_copy(src.at[at], hold.at[at], load_sem.at[n]))
            stores.append(pltpu.make_async_copy(hold.at[at], dst.at[at], store_sem.at[n]))
    for load in loads:
        load.start()
    for load, store in zip(loads, stores):
        load.wait()
        store.start()
    for store in stores:
        store.wait()


def hand_on(arrays):
    hbm = pl.BlockSpec(memory_space=pl.ANY)
    count = sum(len(pieces_of(a)) for a in arrays)
    return pl.pallas_call(
        functools.partial(hand_on_kernel, len(arrays)),
        out_shape=tuple(jax.ShapeDtypeStruct(a.shape, a.dtype) for a in arrays),
        in_specs=[hbm] * len(arrays),
        out_specs=(hbm,) * len(arrays),
        scratch_shapes=[pltpu.VMEM(a.shape, a.dtype) for a in arrays]
        + [pltpu.SemaphoreType.DMA((count,))] * 2,
        compiler_params=pltpu.CompilerParams(vmem_limit_bytes=60 * 2**20),
    )(*arrays)


def local(gate_pre, up_pre, down_weight, block_mask, out_grad):
    blk_rows, blk_cols = block_mask.shape
    ff_local, width = down_weight.shape
    masked = (
        down_weight.reshape(blk_rows, 128, blk_cols, 128)
        * block_mask.astype(jnp.bfloat16)[:, None, :, None]
    ).reshape(ff_local, width)
    gate_val = gate_pre.astype(jnp.float32)
    up_val = up_pre.astype(jnp.float32)
    sigmoid_gate = jax.nn.sigmoid(gate_val)
    silu_gate = gate_val * sigmoid_gate
    hidden = (silu_gate * up_val).astype(jnp.bfloat16)
    layer_out = lax.psum_scatter(
        jnp.dot(hidden, masked, preferred_element_type=jnp.float32),
        "tensor",
        scatter_dimension=0,
        tiled=True,
    ).astype(jnp.bfloat16)
    cot_rows = lax.all_gather(out_grad, "tensor", axis=0, tiled=True)
    hidden_grad = lax.dot_general(
        cot_rows, masked, (((1,), (1,)), ((), ())), preferred_element_type=jnp.float32
    )
    gate_grad = (
        hidden_grad * up_val * sigmoid_gate * (1.0 + gate_val * (1.0 - sigmoid_gate))
    ).astype(jnp.bfloat16)
    up_grad = (hidden_grad * silu_gate).astype(jnp.bfloat16)
    tokens_all = out_grad.shape[0] * lax.axis_size("tensor") * lax.axis_size("dp")
    grad_scale = 1.0 / math.sqrt(tokens_all)
    partial_grad = (
        lax.dot_general(
            hidden, cot_rows, (((0,), (0,)), ((), ())), preferred_element_type=jnp.float32
        )
        * grad_scale
    )
    blocked = (
        partial_grad.reshape(blk_rows, 128, blk_cols, 128)
        * block_mask.astype(jnp.float32)[:, None, :, None]
    )
    summed = lax.psum(blocked.reshape(ff_local, width), "dp")
    weight_grad = summed.astype(jnp.bfloat16)
    return (layer_out, gate_grad, up_grad, weight_grad)


def solution(mesh):
    grouped = mesh.shape["dp"] == 2 and mesh.shape["tensor"] == 16
    return jax.shard_map(
        fused if grouped else local,
        mesh=mesh,
        in_specs=(
            P("dp", "tensor"),
            P("dp", "tensor"),
            P("tensor", None),
            P("tensor", None),
            P(("dp", "tensor"), None),
        ),
        out_specs=(
            P(("dp", "tensor"), None),
            P("dp", "tensor"),
            P("dp", "tensor"),
            P("tensor", None),
        ),
        check_vma=False,
    )
```
